32 devices in a mesh: groups: 1, expert: 16 (over z, y, x), dp: 2 (over core).
Axes of the slice: x: 2, y: 2, z: 4, core: 2. Of those that a mesh axis runs over, the one named last changes fastest.
Arguments:
- tokens: bfloat16 [4096, 2048], P(('groups', 'expert', 'dp')), may hold values from -6 to 6
- routes: int32 [4096, 8], P(('groups', 'expert', 'dp')), may hold values from 0 to 15, all different within a row; in each aligned block of 128 rows (0 to 127, 128 to 255, ...) at most 72 rows name the same one
- route_logits: float32 [4096, 8], P(('groups', 'expert', 'dp')), may hold values from -4 to 4
- cotangent: bfloat16 [4096, 2048], P(('groups', 'expert', 'dp')), may hold values from -6 to 6
- gate_weight: bfloat16 [16, 2048, 768], P('expert', 'dp'), may hold values from -0.125 to 0.125
- up_weight: bfloat16 [16, 2048, 768], P('expert', 'dp'), may hold values from -0.125 to 0.125
- down_weight: bfloat16 [16, 2048, 768], P('expert', 'dp'), may hold values from -0.21875 to 0.21875
Outputs:
- mixed: bfloat16 [4096, 2048], P(('groups', 'expert', 'dp'))
- grad_down: bfloat16 [16, 2048, 768], P(('groups', 'expert'), 'dp')
The draws below stay inside these ranges and needn't reach their ends.
Inputs may be any that keep to these rules, and one draw needn't show every extreme that they name: `routes`: each token names 8 different experts. Within each device's 128 rows (aligned blocks of rows) no expert is named by more than 72 rows, and in some blocks some expert is named by exactly 72. Every expert is named somewhere.
All inputs are finite; a program needn't handle non-finite values.
Results may differ from the reference program's by a relative error of at most 0.0058.
Values may be sent and summed in bfloat16 or wider, within the bound.
No kernel may reach another device: no remote copies, remote signals or barrier semaphores. Data moves between devices by JAX's collectives and lax.ppermute only.
A program may use at most 128 MiB of HBM per device.

```python
import math
import jax
import jax.numpy as jnp
import numpy as np
from jax import lax

D = 2048
FF = 768
DOUT = 2048
TOP = 8
TOK_DEV = 128
EXPERTS = 16
MOST = 72
TOKENS = 4096


def shard_levels(key, extent, split, low, high):
    level, own = 1.0, jax.random.fold_in(key, 6)
    for dim, parts in split:
        heights = jnp.exp(jax.random.uniform(jax.random.fold_in(own, dim), (parts,), jnp.float32, low / len(split), high / len(split)))
        level = level * jnp.repeat(heights, extent[dim] // parts).reshape([-1 if axis == dim else 1 for axis in range(len(extent))])
    return level


def assign_block(own_key, own, number, rows, number_of, top, reach, skew):
    order = jax.random.permutation(own_key, number_of)
    crowded, common = portions_of(number_of, rows * top, reach, skew, True), portions_of(number_of, rows * top, reach, skew, False)
    places = jnp.arange(number_of)

    def named(lengths, turn):
        used = int((lengths > 0).sum())
        fixed = max(1, used // 4)
        passed = fixed + (places - fixed + turn * (used - fixed)) % max(1, number_of - fixed)
        return jnp.zeros((number_of,), jnp.int32).at[order[jnp.where(places < fixed, places, passed)]].set(jnp.asarray(lengths, jnp.int32))

    lengths = jnp.where(number % 4 == 0, named(crowded, number // 4), named(common, number - number // 4 - 1))
    mixed = jax.random.permutation(jax.random.fold_in(own, 3), number_of)
    source_of, taker = mixed[0:number_of // 2 * 2:2], mixed[1:number_of // 2 * 2:2]
    margin = jnp.minimum(lengths[source_of] - 1, reach - lengths[taker]) // 2
    margin = jnp.where((source_of == order[0]) | (taker == order[0]) | (lengths[taker] == 0), 0, jnp.maximum(margin, 0))
    passed = jax.random.randint(jax.random.fold_in(own, 4), (number_of // 2,), 0, 1 << 20) % (margin + 1)
    lengths = lengths.at[source_of].add(-passed).at[taker].add(passed)
    items = jnp.searchsorted(jnp.cumsum(lengths), jnp.arange(rows * top), side="right").astype(jnp.int32)
    table = items.reshape(top, rows).T
    table = table[jax.random.permutation(jax.random.fold_in(own, 1), rows)]
    turn = jax.random.randint(jax.random.fold_in(own, 2), (rows, 1), 0, top)
    return jnp.take_along_axis(table, (jnp.arange(top)[None, :] + turn) % top, axis=1)


def portions_of(count, total, reach, lean, full):
    portions = [(1 << 20) // math.isqrt(grade ** lean) + 1 for grade in range(1, count + 1)]
    largest = reach if full else min(reach, max(-(-total // count), total * portions[0] // sum(portions)))
    least = 1 if total - largest >= count - 1 else 0
    given, spare = [largest] + [least] * (count - 1), total - largest - least * (count - 1)
    while spare > 0:
        free = [i for i in range(1, count) if given[i] < largest] or [i for i in range(1, count) if given[i] < reach]
        pool, left = sum([portions[i] for i in free]), spare
        for i in free:
            more = min(reach - given[i], max(1, left * portions[i] // pool), spare)
            given[i] = given[i] + more
            spare = spare - more
    return np.array(given)


def gaussian(stream_key, extent, scale, limit, shards=(), kind=jnp.bfloat16):
    level = shard_levels(stream_key, extent, shards, -0.22, 0.18) if shards else 1.0
    values = jax.random.normal(stream_key, extent, jnp.float32) * scale * level
    return jnp.minimum(jnp.maximum(values, -limit), limit).astype(kind)


def setup_inputs(seed: int = 0, part: int = 0) -> dict:
    arg_keys = jax.random.split(jax.random.key(seed), 8)
    own_keys = jax.random.split(jax.random.fold_in(arg_keys[7], part), 8)
    tokens = gaussian(own_keys[0], (TOKENS, D), 1.0, 6.0, ((0, 32),))
    routes_keys = jax.random.split(jax.random.fold_in(own_keys[1], 1), TOKENS // TOK_DEV)
    routes_turns = jax.random.permutation(jax.random.fold_in(own_keys[1], 3), TOKENS // TOK_DEV)
    routes = jax.vmap(lambda own, number: assign_block(jax.random.fold_in(own_keys[1], 2), own, number, TOK_DEV, EXPERTS, TOP, MOST, 2))(routes_keys, routes_turns).reshape((TOKENS, TOP))
    route_logits = gaussian(own_keys[2], (TOKENS, TOP), 1.0, 4.0, ((0, 32),), jnp.float32)
    cotangent = gaussian(own_keys[3], (TOKENS, DOUT), 1.0, 6.0, ((0, 32),))
    gate_weight = gaussian(arg_keys[4], (EXPERTS, D, FF), D ** -0.5, 0.125, ((0, 16), (1, 2)))
    up_weight = gaussian(arg_keys[5], (EXPERTS, D, FF), D ** -0.5, 0.125, ((0, 16), (1, 2)))
    down_weight = gaussian(arg_keys[6], (EXPERTS, DOUT, FF), FF ** -0.5, 0.21875, ((0, 16), (1, 2)))
    return dict(tokens=tokens, routes=routes, route_logits=route_logits, cotangent=cotangent, gate_weight=gate_weight, up_weight=up_weight, down_weight=down_weight)


def reference(tokens, routes, route_logits, cotangent, gate_weight, up_weight, down_weight):
    devices = TOKENS // TOK_DEV
    pair_block = TOK_DEV * TOP
    pair_total = TOKENS * TOP
    exp_logits = jnp.exp(route_logits)
    route_weight = exp_logits / jnp.sum(exp_logits, axis=1, keepdims=True)
    blocks = routes.reshape(devices, pair_block).astype(jnp.int32)
    onehot = (blocks[:, :, None] == jnp.arange(EXPERTS, dtype=jnp.int32)[None, None, :]).astype(jnp.int32)
    position = jnp.sum((jnp.cumsum(onehot, axis=1) - onehot) * onehot, axis=2).astype(jnp.int32)
    device_ids = jnp.broadcast_to(jnp.arange(devices, dtype=jnp.int32)[:, None], (devices, pair_block))
    pair_ids = jnp.arange(pair_total, dtype=jnp.int32).reshape(devices, pair_block)
    table = jnp.full((EXPERTS, devices, MOST), pair_total, jnp.int32)
    table = table.at[blocks, device_ids, position].set(pair_ids)
    padded_tokens = jnp.concatenate([tokens, jnp.zeros((1, D), tokens.dtype)], axis=0)
    padded_cot = jnp.concatenate([cotangent, jnp.zeros((1, DOUT), cotangent.dtype)], axis=0)
    padded_weight = jnp.concatenate([route_weight.reshape(-1), jnp.zeros((1,), jnp.float32)], axis=0)

    def per_expert(carry, inputs):
        expert_table, gate_mat, up_mat, down_mat = inputs
        pair_index = expert_table.reshape(-1)
        token_index = (pair_index // TOP).astype(jnp.int32)
        rows = padded_tokens[token_index]
        gate_act = jnp.dot(rows, gate_mat, preferred_element_type=jnp.float32)
        up_act = jnp.dot(rows, up_mat, preferred_element_type=jnp.float32)
        hidden = (jax.nn.silu(gate_act) * up_act).astype(jnp.bfloat16)
        outputs = lax.dot_general(hidden, down_mat, (((1,), (1,)), ((), ())), preferred_element_type=jnp.float32).astype(jnp.bfloat16)
        weight = padded_weight[pair_index]
        carry = carry.at[token_index].add(weight[:, None] * outputs.astype(jnp.float32))
        out_grad = (weight[:, None] * padded_cot[token_index].astype(jnp.float32)).astype(jnp.bfloat16)
        grad = lax.dot_general(out_grad, hidden, (((0,), (0,)), ((), ())), preferred_element_type=jnp.float32)
        return carry, grad.astype(jnp.bfloat16)

    total, grad_down = lax.scan(per_expert, jnp.zeros((TOKENS + 1, DOUT), jnp.float32), (table, gate_weight, up_weight, down_weight))
    return total[:TOKENS].astype(jnp.bfloat16), grad_down
```

```python
import functools

import jax
import jax.numpy as jnp
from jax import lax
from jax.experimental import pallas as pl
from jax.experimental.pallas import tpu as pltpu
from jax.sharding import PartitionSpec as P

F32 = jnp.float32
BF16 = jnp.bfloat16
VMEM_LIMIT = 48 * 1024 * 1024


def two_levels(experts):
    minor = 1
    while minor * minor * 4 <= experts:
        minor *= 2
    return experts // minor, minor


def column_tile(columns):
    return 512 if columns % 512 == 0 else columns


def select_kernel(peers, count, slots, scaled, pos_ref, weight_ref, *refs):
    sources, outs = refs[:count], refs[count:]
    toks = pos_ref.shape[1]
    slot = lax.broadcasted_iota(jnp.int32, (slots, toks), 0).astype(F32)
    for g in range(count):
        hits = [slot == pos_ref[k * count + g : k * count + g + 1, :] for k in range(peers)]
        onehot = jnp.concatenate([jnp.where(h, 1.0, 0.0) for h in hits], axis=0).astype(BF16)
        rows = jnp.dot(onehot, sources[g][...], preferred_element_type=F32)
        for k in range(peers):
            part = rows[k * slots : (k + 1) * slots]
            if scaled:
                weights = weight_ref[k * count + g : k * count + g + 1, :]
                part = part * jnp.sum(jnp.where(hits[k], weights, 0.0), axis=1, keepdims=True)
            outs[k][g] = part.astype(BF16)


def select(pos, weight, sources, slots, scaled):
    count = len(sources)
    peers = pos.shape[0] // count
    toks, cols = sources[0].shape
    tile = column_tile(cols)
    small = pl.BlockSpec(pos.shape, lambda j: (0, 0))
    return pl.pallas_call(
        functools.partial(select_kernel, peers, count, slots, scaled),
        grid=(cols // tile,),
        in_specs=[small, small] + [pl.BlockSpec((toks, tile), lambda j: (0, j))] * count,
        out_specs=[pl.BlockSpec((count, slots, tile), lambda j: (0, 0, j))] * peers,
        out_shape=[jax.ShapeDtypeStruct((count, slots, cols), BF16)] * peers,
        compiler_params=pltpu.CompilerParams(vmem_limit_bytes=VMEM_LIMIT),
        cost_estimate=pl.CostEstimate(
            flops=2 * peers * count * slots * toks * cols,
            bytes_accessed=2 * count * cols * (toks + peers * slots),
            transcendentals=0,
        ),
    )(pos, weight, *sources)


def combine_kernel(peers, count, extra, pos_ref, weight_ref, *refs):
    rows, extras, outs = refs[:peers], refs[peers : peers + extra], refs[peers + extra :]
    toks = pos_ref.shape[1]
    slots = rows[0].shape[1]
    slot = lax.broadcasted_iota(jnp.int32, (slots, toks), 0).astype(F32)
    across = (((0,), (0,)), ((), ()))
    for g in range(count):
        total = None
        for k in range(peers):
            at = slice(k * count + g, k * count + g + 1)
            spread = jnp.where(slot == pos_ref[at, :], weight_ref[at, :], 0.0)
            high = spread.astype(BF16)
            low = (spread - high.astype(F32)).astype(BF16)
            part = rows[k][g]
            part = lax.dot_general(
                high, part, across, preferred_element_type=F32
            ) + lax.dot_general(low, part, across, preferred_element_type=F32)
            total = part if total is None else total + part
        for e in extras:
            total = total + e[...].astype(F32)
        outs[g][...] = total.astype(BF16)


def combine(pos, weight, rows, extras=()):
    count, slots, cols = rows[0].shape
    peers, toks = len(rows), pos.shape[1]
    tile = column_tile(cols)
    small = pl.BlockSpec(pos.shape, lambda j: (0, 0))
    flat = pl.BlockSpec((toks, tile), lambda j: (0, j))
    return pl.pallas_call(
        functools.partial(combine_kernel, peers, count, len(extras)),
        grid=(cols // tile,),
        in_specs=[small, small]
        + [pl.BlockSpec((count, slots, tile), lambda j: (0, 0, j))] * peers
        + [flat] * len(extras),
        out_specs=[flat] * count,
        out_shape=[jax.ShapeDtypeStruct((toks, cols), BF16)] * count,
        compiler_params=pltpu.CompilerParams(vmem_limit_bytes=VMEM_LIMIT),
        cost_estimate=pl.CostEstimate(
            flops=4 * peers * count * slots * toks * cols,
            bytes_accessed=2 * cols * (count * (toks + peers * slots) + toks * len(extras)),
            transcendentals=0,
        ),
    )(pos, weight, *rows, *extras)


def shards(tokens, routes, route_logits, cotangent, gate_weight, up_weight, down_weight):
    toks, top = routes.shape
    experts = lax.axis_size("expert")
    major, minor = two_levels(experts)
    per_expert = toks * top // experts
    slots = min(toks, per_expert + max(2, per_expert // 8))
    slots = -(-slots // 8) * 8
    here = lax.axis_index("expert")
    core = lax.axis_index("dp")
    plane, place = here // minor, here % minor

    def to_plane(x, shift):
        return lax.ppermute(x, "expert", [(i, (i + shift * minor) % experts) for i in range(experts)])

    def to_peer(x, k):
        return lax.ppermute(x, "expert", [(i, i ^ k) for i in range(experts)])

    def other_core(x):
        return lax.ppermute(x, "dp", [(0, 1), (1, 0)])

    exp_logits = jnp.exp(route_logits)
    route_weight = (exp_logits / jnp.sum(exp_logits, axis=1, keepdims=True)).T
    names = routes.T[:, None, :] == jnp.arange(experts, dtype=jnp.int32)[None, :, None]
    chosen = jnp.sum(names.astype(F32), axis=0)
    dense_weight = jnp.sum(jnp.where(names, route_weight[:, None, :], 0.0), axis=0)
    before = jnp.arange(toks)[:, None] < jnp.arange(toks)[None, :]
    position = jnp.dot(chosen.astype(BF16), before.astype(BF16), preferred_element_type=F32)
    meta = jnp.stack([jnp.where(chosen > 0, position, -1.0), dense_weight])

    metas = [meta] + [to_plane(meta, s) for s in range(1, major)]
    token_rows = [tokens] + [to_plane(tokens, s) for s in range(1, major)]
    cot_rows = [cotangent] + [to_plane(cotangent, s) for s in range(1, major)]

    mine = plane * minor + (place ^ jnp.arange(minor))
    mine = (mine[:, None] == jnp.arange(experts)[None, :]).astype(F32)

    groups = []
    for near in range(major // 2 + 1):
        groups.append(sorted({near, (major - near) % major}))

    def full_of(w):
        w = w[0]
        got = other_core(w)
        return jnp.concatenate([jnp.where(core == 0, w, got), jnp.where(core == 0, got, w)], axis=0)

    gate_mat, up_mat, down_mat = full_of(gate_weight), full_of(up_weight), full_of(down_weight)

    tables, hiddens, grads, returns = [], [], [], []
    for shifts in groups:
        stacked = jnp.stack([metas[s] for s in shifts])
        picked = jnp.sum(stacked[:, :, None] * mine[None, None, :, :, None], axis=3)
        picked = picked.transpose(1, 2, 0, 3).reshape(2, minor * len(shifts), toks)
        pos, weight = picked[0], picked[1]
        tables.append((pos, weight))
        rows = select(pos, weight, [token_rows[s] for s in shifts], slots, False)
        rows = [rows[0]] + [to_peer(rows[k], k) for k in range(1, minor)]
        flat = jnp.concatenate(rows, axis=0).reshape(-1, tokens.shape[1])
        gate_act = jnp.dot(flat, gate_mat, preferred_element_type=F32)
        up_act = jnp.dot(flat, up_mat, preferred_element_type=F32)
        hidden = (jax.nn.silu(gate_act) * up_act).astype(BF16)
        hiddens.append(hidden)
    for shifts, (pos, weight) in zip(groups, tables):
        rows = select(pos, weight, [cot_rows[s] for s in shifts], slots, True)
        rows = [rows[0]] + [to_peer(rows[k], k) for k in range(1, minor)]
        grads.append(jnp.concatenate(rows, axis=0).reshape(-1, cotangent.shape[1]))

    partial = []
    for shifts, (pos, weight), hidden in reversed(list(zip(groups, tables, hiddens))):
        out = lax.dot_general(
            hidden, down_mat, (((1,), (1,)), ((), ())), preferred_element_type=F32
        ).astype(BF16)
        out = out.reshape(minor, len(shifts), slots, out.shape[1])
        rows = [out[0]] + [to_peer(out[k], k) for k in range(1, minor)]
        if shifts != [0]:
            sums = combine(pos, weight, rows)
            partial += [to_plane(x, major - s) for s, x in zip(shifts, sums)]
        else:
            (mixed,) = combine(pos, weight, rows, partial)

    hidden_all = jnp.concatenate(hiddens, axis=0)
    grad_all = jnp.concatenate(grads, axis=0)
    half = grad_all.shape[1] // 2
    over_rows = (((0,), (0,)), ((), ()))

    def grad_of(which):
        side = lax.dynamic_slice_in_dim(grad_all, which * half, half, axis=1)
        return lax.dot_general(side, hidden_all, over_rows, preferred_element_type=F32)

    theirs = other_core(grad_of(1 - core).astype(BF16))
    grad = (grad_of(core) + theirs.astype(F32)).astype(BF16)
    return mixed, grad[None]


def solution(mesh):
    placed = (
        P(("groups", "expert", "dp"), None),
        P(("groups", "expert", "dp"), None),
        P(("groups", "expert", "dp"), None),
        P(("groups", "expert", "dp"), None),
        P("expert", "dp", None),
        P("expert", "dp", None),
        P("expert", "dp", None),
    )
    return jax.shard_map(
        shards,
        mesh=mesh,
        in_specs=placed,
        out_specs=(P(("groups", "expert", "dp"), None), P(("groups", "expert"), "dp", None)),
        check_vma=False,
    )
```

```python
import functools

import jax
import jax.numpy as jnp
from jax import lax
from jax.experimental import pallas as pl
from jax.experimental.pallas import tpu as pltpu
from jax.sharding import PartitionSpec as P

F32 = jnp.float32
BF16 = jnp.bfloat16
VMEM_LIMIT = 48 * 1024 * 1024
DEPTH = 1


def two_levels(experts):
    minor = 1
    while minor * minor * 4 <= experts:
        minor *= 2
    return experts // minor, minor


def column_tile(columns):
    return 512 if columns % 512 == 0 else columns


def select_kernel(peers, count, slots, scaled, _, pos_ref, weight_ref, *refs):
    sources, outs = refs[:count], refs[count:]
    toks = pos_ref.shape[1]
    slot = lax.broadcasted_iota(jnp.int32, (slots, toks), 0).astype(F32)
    for g in range(count):
        hits = [slot == pos_ref[k * count + g : k * count + g + 1, :] for k in range(peers)]
        onehot = jnp.concatenate([jnp.where(h, 1.0, 0.0) for h in hits], axis=0).astype(BF16)
        rows = jnp.dot(onehot, sources[g][0], preferred_element_type=F32)
        for k in range(peers):
            part = rows[k * slots : (k + 1) * slots]
            if scaled:
                weights = weight_ref[k * count + g : k * count + g + 1, :]
                part = part * jnp.sum(jnp.where(hits[k], weights, 0.0), axis=1, keepdims=True)
            outs[k][g] = part.astype(BF16)


def select(plane, shifts, pos, weight, blocks, slots, scaled):
    count = len(shifts)
    peers = pos.shape[0] // count
    major, toks, cols = blocks.shape
    tile = column_tile(cols)
    small = pl.BlockSpec(pos.shape, lambda j, ref: (0, 0))

    def source(shift):
        return pl.BlockSpec(
            (1, toks, tile), lambda j, ref: (lax.rem(ref[0] + (major - shift), major), 0, j)
        )

    return pl.pallas_call(
        functools.partial(select_kernel, peers, count, slots, scaled),
        grid_spec=pltpu.PrefetchScalarGridSpec(
            num_scalar_prefetch=1,
            grid=(cols // tile,),
            in_specs=[small, small] + [source(shift) for shift in shifts],
            out_specs=[pl.BlockSpec((count, slots, tile), lambda j, ref: (0, 0, j))] * peers,
        ),
        out_shape=[jax.ShapeDtypeStruct((count, slots, cols), BF16)] * peers,
        compiler_params=pltpu.CompilerParams(vmem_limit_bytes=VMEM_LIMIT),
        cost_estimate=pl.CostEstimate(
            flops=2 * peers * count * slots * toks * cols,
            bytes_accessed=2 * count * cols * (toks + peers * slots),
            transcendentals=0,
        ),
    )(plane.reshape(1), pos, weight, *[blocks] * count)


def combine_kernel(peers, _, pos_ref, weight_ref, *refs):
    rows, out = refs[:peers], refs[peers]
    g, count = pl.program_id(0), pl.num_programs(0)
    toks, slots = pos_ref.shape[1], rows[0].shape[1]
    slot = lax.broadcasted_iota(jnp.int32, (slots, toks), 0).astype(F32)
    across = (((0,), (0,)), ((), ()))
    total = None
    for k in range(peers):
        at = pl.ds(k * count + g, 1)
        spread = jnp.where(slot == pos_ref[at, :], weight_ref[at, :], 0.0)
        high = spread.astype(BF16)
        low = (spread - high.astype(F32)).astype(BF16)
        part = rows[k][0]
        part = lax.dot_general(
            high, part, across, preferred_element_type=F32
        ) + lax.dot_general(low, part, across, preferred_element_type=F32)
        total = part if total is None else total + part
    out[0] = total.astype(BF16)


def combine(plane, pos, weight, rows):
    count, slots, cols = rows[0].shape
    peers, toks = len(rows), pos.shape[1]
    small = pl.BlockSpec(pos.shape, lambda g, ref: (0, 0))
    return pl.pallas_call(
        functools.partial(combine_kernel, peers),
        grid_spec=pltpu.PrefetchScalarGridSpec(
            num_scalar_prefetch=1,
            grid=(count,),
            in_specs=[small, small]
            + [pl.BlockSpec((1, slots, cols), lambda g, ref: (g, 0, 0))] * peers,
            out_specs=pl.BlockSpec(
                (1, toks, cols), lambda g, ref: (lax.rem(ref[0] + count - g, count), 0, 0)
            ),
        ),
        out_shape=jax.ShapeDtypeStruct((count, toks, cols), BF16),
        compiler_params=pltpu.CompilerParams(vmem_limit_bytes=VMEM_LIMIT),
        cost_estimate=pl.CostEstimate(
            flops=4 * peers * count * slots * toks * cols,
            bytes_accessed=2 * cols * count * (toks + peers * slots),
            transcendentals=0,
        ),
    )(plane.reshape(1), pos, weight, *rows)


def shards(tokens, routes, route_logits, cotangent, gate_weight, up_weight, down_weight):
    toks, top = routes.shape
    experts = lax.axis_size("expert")
    major, minor = two_levels(experts)
    per_expert = toks * top // experts
    slots = min(toks, per_expert + max(2, per_expert // 8))
    slots = -(-slots // 8) * 8
    here = lax.axis_index("expert")
    core = lax.axis_index("dp")
    plane, place = here // minor, here % minor

    def to_plane(x, shift):
        return lax.ppermute(x, "expert", [(i, (i + shift * minor) % experts) for i in range(experts)])

    def to_peer(x, k):
        return lax.ppermute(x, "expert", [(i, i ^ k) for i in range(experts)])

    def other_core(x):
        return lax.ppermute(x, "dp", [(0, 1), (1, 0)])

    def after(x, earlier):
        return lax.optimization_barrier((x, *earlier))[0] if earlier else x

    exp_logits = jnp.exp(route_logits)
    route_weight = (exp_logits / jnp.sum(exp_logits, axis=1, keepdims=True)).T
    names = routes.T[:, None, :] == jnp.arange(experts, dtype=jnp.int32)[None, :, None]
    chosen = jnp.sum(names.astype(F32), axis=0)
    dense_weight = jnp.sum(jnp.where(names, route_weight[:, None, :], 0.0), axis=0)
    before = jnp.arange(toks)[:, None] < jnp.arange(toks)[None, :]
    position = jnp.dot(chosen.astype(BF16), before.astype(BF16), preferred_element_type=F32)
    meta = jnp.stack([jnp.where(chosen > 0, position, -1.0), dense_weight])

    mine = plane * minor + (place ^ jnp.arange(minor))
    mine = (mine[:, None] == jnp.arange(experts)[None, :]).astype(F32)

    same_place = [[i * minor + j for i in range(major)] for j in range(minor)]

    def spread(x):
        return lax.all_gather(x, "expert", axis=0, axis_index_groups=same_place)

    model_width, out_cols = tokens.shape[1], cotangent.shape[1]
    piece = out_cols // 4
    cot_parts = [
        jnp.concatenate([cotangent[:, h * piece : (h + 1) * piece], cotangent[:, (2 + h) * piece : (3 + h) * piece]], axis=1)
        for h in range(2)
    ]
    token_parts = [tokens[:, : model_width // 2], tokens[:, model_width // 2 :]]
    token_all = [spread(x) for x in token_parts]
    cot_all = [spread(x) for x in cot_parts]

    metas = [meta] + [to_plane(meta, s) for s in range(1, major)]

    def table_of(shifts):
        stacked = jnp.stack([metas[s] for s in shifts])
        picked = jnp.sum(stacked[:, :, None] * mine[None, None, :, :, None], axis=3)
        picked = picked.transpose(1, 2, 0, 3).reshape(2, minor * len(shifts), toks)
        return picked[0], picked[1]

    all_table = table_of(list(range(major)))
    by_peer = [t.reshape(minor, major, toks) for t in all_table]
    own_table = [t[:, 0] for t in by_peer]
    rest_table = [t[:, 1:].reshape(-1, toks) for t in by_peer]
    others = list(range(1, major))

    def full_of(w, *earlier):
        w = w[0]
        got = other_core(after(w, earlier))
        return jnp.concatenate([jnp.where(core == 0, w, got), jnp.where(core == 0, got, w)], axis=0)

    gate_mat, up_mat = full_of(gate_weight, *metas[1:]), full_of(up_weight, *metas[1:])
    down_mat = full_of(down_weight, gate_mat)

    queues = [[] for _ in range(minor)]

    def exchange(rows):
        got = [rows[0]]
        for k in range(1, minor):
            queue = queues[k]
            got.append(to_peer(after(rows[k], queue[-DEPTH:][:1] if len(queue) >= DEPTH else []), k))
            queue.append(got[k])
        return got

    def send_own(x, scaled, *earlier):
        blocks = after(x, earlier)[None]
        here_only = jnp.zeros((), jnp.int32)
        return exchange(select(here_only, [0], *own_table, blocks, slots, scaled))

    def send_rest(blocks, scaled):
        return exchange(select(plane, others, *rest_table, blocks, slots, scaled))

    def joined(parts):
        return jnp.concatenate(parts, axis=0).reshape(-1, parts[0].shape[-1])

    def hidden_of(pieces):
        def against(w):
            total, at = None, 0
            for x in pieces:
                part = jnp.dot(x, w[at : at + x.shape[1]], preferred_element_type=F32)
                total, at = part if total is None else total + part, at + x.shape[1]
            return total

        return (jax.nn.silu(against(gate_mat)) * against(up_mat)).astype(BF16)

    own_rows = joined(send_own(tokens, False))
    own_hidden = hidden_of([own_rows])
    blocks = after(token_all[0], (gate_mat, up_mat, down_mat))
    first = send_rest(blocks, False)
    second = send_rest(after(token_all[1], first[1:]), False)
    rest_rows = [joined(first), joined(second)]
    own_cots = joined(send_own(jnp.concatenate(cot_parts, axis=1), True))
    rest_hidden = hidden_of(rest_rows)

    hidden = jnp.concatenate(
        [own_hidden.reshape(minor, 1, slots, -1), rest_hidden.reshape(minor, major - 1, slots, -1)],
        axis=1,
    ).reshape(minor * major * slots, -1)
    wide = out_cols // 2
    outs = [
        lax.dot_general(
            hidden,
            down_mat[h * wide : (h + 1) * wide],
            (((1,), (1,)), ((), ())),
            preferred_element_type=F32,
        ).astype(BF16).reshape(minor, major, slots, wide)
        for h in range(2)
    ]
    mixed = []
    for h in range(2):
        back = exchange([outs[h][k] for k in range(minor)])
        sums = combine(plane, *all_table, [after(x, [outs[1]]) for x in back])
        mixed.append(
            lax.psum_scatter(sums, "expert", scatter_dimension=0, axis_index_groups=same_place)
        )
    mixed = jnp.concatenate(mixed, axis=1)
    rest_cots = [joined(send_rest(x, True)) for x in cot_all]

    over_rows = (((0,), (0,)), ((), ()))
    done = []
    for h in range(2):
        own_half = own_cots[:, h * 2 * piece : (h + 1) * 2 * piece]

        def grad_of(which):
            def part(rows, hidden):
                side = lax.dynamic_slice_in_dim(rows, which * piece, piece, axis=1)
                return lax.dot_general(side, hidden, over_rows, preferred_element_type=F32)

            return part(own_half, own_hidden) + part(rest_cots[h], rest_hidden)

        theirs = other_core(grad_of(1 - core).astype(BF16))
        done.append((grad_of(core) + theirs.astype(F32)).astype(BF16))
    return mixed, jnp.concatenate(done, axis=0)[None]


def solution(mesh):
    placed = (
        P(("groups", "expert", "dp"), None),
        P(("groups", "expert", "dp"), None),
        P(("groups", "expert", "dp"), None),
        P(("groups", "expert", "dp"), None),
        P("expert", "dp", None),
        P("expert", "dp", None),
        P("expert", "dp", None),
    )
    return jax.shard_map(
        shards,
        mesh=mesh,
        in_specs=placed,
        out_specs=(P(("groups", "expert", "dp"), None), P(("groups", "expert"), "dp", None)),
        check_vma=False,
    )
```

```python
import functools

import jax
import jax.numpy as jnp
from jax import lax
from jax.experimental import pallas as pl
from jax.experimental.pallas import tpu as pltpu
from jax.sharding import PartitionSpec as P

F32 = jnp.float32
BF16 = jnp.bfloat16
VMEM_LIMIT = 48 * 1024 * 1024


def two_levels(experts):
    minor = 1
    while minor * minor * 4 <= experts:
        minor *= 2
    return experts // minor, minor


def column_tile(columns):
    return 512 if columns % 512 == 0 else columns


def select_kernel(peers, count, slots, scaled, _, pos_ref, weight_ref, *refs):
    sources, outs = refs[:count], refs[count:]
    toks = pos_ref.shape[1]
    slot = lax.broadcasted_iota(jnp.int32, (slots, toks), 0).astype(F32)
    for g in range(count):
        hits = [slot == pos_ref[k * count + g : k * count + g + 1, :] for k in range(peers)]
        onehot = jnp.concatenate([jnp.where(h, 1.0, 0.0) for h in hits], axis=0).astype(BF16)
        rows = jnp.dot(onehot, sources[g][0], preferred_element_type=F32)
        for k in range(peers):
            part = rows[k * slots : (k + 1) * slots]
            if scaled:
                weights = weight_ref[k * count + g : k * count + g + 1, :]
                part = part * jnp.sum(jnp.where(hits[k], weights, 0.0), axis=1, keepdims=True)
            outs[k][g] = part.astype(BF16)


def select(blocks, which, table, slots, scaled, tiles, tile):
    pos, weight = table
    count = len(blocks)
    peers = pos.shape[0] // count
    toks = blocks[0].shape[1]
    cols = tile * len(tiles)
    small = pl.BlockSpec(pos.shape, lambda j, ref: (0, 0))
    step = tiles[1] - tiles[0] if len(tiles) > 1 else 1
    inner = next((i for i in range(1, len(tiles)) if tiles[i] - tiles[i - 1] != step), len(tiles))
    hop = tiles[inner] - tiles[0] if inner < len(tiles) else 0

    def column(j):
        return tiles[0] + lax.rem(j, inner) * step + (j // inner) * hop

    def source(g):
        return pl.BlockSpec((1, toks, tile), lambda j, ref: (ref[g], 0, column(j)))

    return pl.pallas_call(
        functools.partial(select_kernel, peers, count, slots, scaled),
        grid_spec=pltpu.PrefetchScalarGridSpec(
            num_scalar_prefetch=1,
            grid=(len(tiles),),
            in_specs=[small, small] + [source(g) for g in range(count)],
            out_specs=[pl.BlockSpec((count, slots, tile), lambda j, ref: (0, 0, j))] * peers,
        ),
        out_shape=[jax.ShapeDtypeStruct((count, slots, cols), BF16)] * peers,
        compiler_params=pltpu.CompilerParams(vmem_limit_bytes=VMEM_LIMIT),
        cost_estimate=pl.CostEstimate(
            flops=2 * peers * count * slots * toks * cols,
            bytes_accessed=2 * count * cols * (toks + peers * slots),
            transcendentals=0,
        ),
    )(which, pos, weight, *blocks)


def combine_kernel(peers, _, pos_ref, weight_ref, *refs):
    own, rest, out = refs[:peers], refs[peers : 2 * peers], refs[2 * peers]
    g, count = pl.program_id(0), pl.num_programs(0)
    toks, slots = pos_ref.shape[1], own[0].shape[1]

    def add_up(rows):
        slot = lax.broadcasted_iota(jnp.int32, (slots, toks), 0).astype(F32)
        spread = []
        for k in range(peers):
            at = pl.ds(k * count + g, 1)
            spread.append(jnp.where(slot == pos_ref[at, :], weight_ref[at, :], 0.0))
        spread = jnp.concatenate(spread, axis=0)
        high = spread.astype(BF16).astype(F32)
        both = jnp.concatenate([high, spread - high], axis=1).astype(BF16)
        held = jnp.concatenate([r[0] for r in rows], axis=0)
        total = lax.dot_general(both, held, (((0,), (0,)), ((), ())), preferred_element_type=F32)
        out[0] = (total[:toks] + total[toks:]).astype(BF16)

    pl.when(g == 0)(lambda: add_up(own))
    pl.when(g > 0)(lambda: add_up(rest))


def combine(which, table, own, rest, half):
    pos, weight = table
    count, slots, cols = rest[0].shape
    count += 1
    peers, toks = len(rest), pos.shape[1]
    small = pl.BlockSpec(pos.shape, lambda g, ref: (0, 0))
    return pl.pallas_call(
        functools.partial(combine_kernel, peers),
        grid_spec=pltpu.PrefetchScalarGridSpec(
            num_scalar_prefetch=1,
            grid=(count,),
            in_specs=[small, small]
            + [pl.BlockSpec((1, slots, cols), lambda g, ref: (0, 0, half))] * peers
            + [pl.BlockSpec((1, slots, cols), lambda g, ref: (jnp.maximum(g - 1, 0), 0, 0))] * peers,
            out_specs=pl.BlockSpec((1, toks, cols), lambda g, ref: (ref[g], 0, 0)),
        ),
        out_shape=jax.ShapeDtypeStruct((count, toks, cols), BF16),
        compiler_params=pltpu.CompilerParams(vmem_limit_bytes=VMEM_LIMIT),
        cost_estimate=pl.CostEstimate(
            flops=4 * peers * count * slots * toks * cols,
            bytes_accessed=2 * cols * count * (toks + peers * slots),
            transcendentals=0,
        ),
    )(which, pos, weight, *own, *rest)


def shards(tokens, routes, route_logits, cotangent, gate_weight, up_weight, down_weight):
    toks, top = routes.shape
    experts = lax.axis_size("expert")
    major, minor = two_levels(experts)
    per_expert = toks * top // experts
    slots = min(toks, per_expert + max(2, per_expert // 8))
    slots = -(-slots // 8) * 8
    here = lax.axis_index("expert")
    core = lax.axis_index("dp")
    plane, place = here // minor, here % minor

    def to_plane(x, shift):
        return lax.ppermute(x, "expert", [(i, (i + shift * minor) % experts) for i in range(experts)])

    def to_peer(x, k):
        return lax.ppermute(x, "expert", [(i, i ^ k) for i in range(experts)])

    def other_core(x):
        return lax.ppermute(x, "dp", [(0, 1), (1, 0)])

    def after(x, earlier):
        return lax.optimization_barrier((x, *earlier))[0] if earlier else x

    def after_all(xs, earlier):
        return list(lax.optimization_barrier((*xs, *earlier))[: len(xs)])

    exp_logits = jnp.exp(route_logits)
    route_weight = (exp_logits / jnp.sum(exp_logits, axis=1, keepdims=True)).T
    names = routes.T[:, None, :] == jnp.arange(experts, dtype=jnp.int32)[None, :, None]
    chosen = jnp.sum(names.astype(F32), axis=0)
    dense_weight = jnp.sum(jnp.where(names, route_weight[:, None, :], 0.0), axis=0)
    before = jnp.arange(toks)[:, None] < jnp.arange(toks)[None, :]
    position = jnp.dot(chosen.astype(BF16), before.astype(BF16), preferred_element_type=F32)
    meta = jnp.stack([jnp.where(chosen > 0, position, -1.0), dense_weight])

    mine = plane * minor + (place ^ jnp.arange(minor))
    mine = (mine[:, None] == jnp.arange(experts)[None, :]).astype(F32)

    sender = (plane + major - jnp.arange(major, dtype=jnp.int32)) % major
    zero = jnp.zeros((1,), jnp.int32)
    same_place = [[i * minor + j for i in range(major)] for j in range(minor)]
    model_width, out_cols = tokens.shape[1], cotangent.shape[1]
    piece, wide, deep = out_cols // 4, out_cols // 2, model_width // 2

    def spread(x):
        return lax.all_gather(x, "expert", axis=0, axis_index_groups=same_place)

    token_all = [spread(tokens[:, h * deep : (h + 1) * deep]) for h in range(2)]
    cot_all = [
        spread(
            jnp.concatenate(
                [cotangent[:, i * piece : (i + 1) * piece] for i in (h, 2 + h)], axis=1
            )
        )
        for h in range(2)
    ]
    metas = [meta] + [to_plane(meta, s) for s in range(1, major)]

    def table_of(shifts):
        stacked = jnp.stack([metas[s] for s in shifts])
        picked = jnp.sum(stacked[:, :, None] * mine[None, None, :, :, None], axis=3)
        picked = picked.transpose(1, 2, 0, 3).reshape(2, minor * len(shifts), toks)
        return picked[0], picked[1]

    own_table, all_table = table_of([0]), table_of(list(range(major)))
    rest_table = [t.reshape(minor, major, toks)[:, 1:].reshape(-1, toks) for t in all_table]

    queue = [[] for _ in range(minor)]

    def exchange(rows):
        back = [rows[0]]
        for k in range(1, minor):
            back.append(to_peer(after(rows[k], queue[k]), k))
            queue[k] = [back[k]]
        return back

    def joined(parts):
        return jnp.concatenate(parts, axis=0).reshape(-1, parts[0].shape[-1])

    def pick_rest(x, scaled):
        tile = column_tile(x.shape[2])
        tiles = list(range(x.shape[2] // tile))
        return select([x] * (major - 1), sender[1:], rest_table, slots, scaled, tiles, tile)

    def hidden_of(pieces):
        def against(w):
            total, at = None, 0
            for x in pieces:
                part = jnp.dot(x, w[at : at + x.shape[1]], preferred_element_type=F32)
                total, at = part if total is None else total + part, at + x.shape[1]
            return total

        return (jax.nn.silu(against(gate_mat)) * against(up_mat)).astype(BF16)

    def out_of(hidden, w):
        out = lax.dot_general(hidden, w, (((1,), (1,)), ((), ())), preferred_element_type=F32)
        out = out.astype(BF16).reshape(minor, -1, slots, w.shape[0])
        return [out[k] for k in range(minor)]

    tile = column_tile(model_width)
    got = [other_core(w[0]) for w in (gate_weight, up_weight, down_weight)]
    gate_mat, up_mat, down_mat = (
        jnp.concatenate([jnp.where(core == 0, w[0], g), jnp.where(core == 0, g, w[0])], axis=0)
        for w, g in zip((gate_weight, up_weight, down_weight), got)
    )
    every = list(range(model_width // tile))
    own_tokens = after(tokens, metas[1:])[None]
    own_rows = exchange(select([own_tokens], zero, own_table, slots, False, every, tile))
    own_cots = joined(
        exchange(select([cotangent[None]], zero, own_table, slots, True, [0, 2, 1, 3], piece))
    )
    own_hidden = hidden_of([joined(own_rows)])
    own_out = out_of(own_hidden, down_mat)
    first = exchange(pick_rest(after(token_all[0], got), False))
    second = exchange(pick_rest(after(token_all[1], [*first[1:], *own_out]), False))
    own_back = exchange(own_out)
    rest_hidden = hidden_of([joined(first), joined(second)])

    outs = [out_of(rest_hidden, down_mat[h * wide : (h + 1) * wide]) for h in range(2)]
    cots = [pick_rest(after(cot_all[0], second[1:]), True), None]
    mixed = []
    for h in range(2):
        back = exchange(outs[h] if h else after_all(outs[h], cots[0]))
        sums = combine(sender, all_table, own_back, after_all(back, outs[1]), h)
        mixed.append(
            lax.psum_scatter(sums, "expert", scatter_dimension=0, axis_index_groups=same_place)
        )
    mixed = jnp.concatenate(mixed, axis=1)
    cots[1] = pick_rest(cot_all[1], True)
    rest_cots = [joined(exchange(x)) for x in cots]

    over_rows = (((0,), (0,)), ((), ()))
    done = []
    for h in range(2):
        own_half = own_cots[:, h * 2 * piece : (h + 1) * 2 * piece]

        def grad_of(which):
            def part(rows, hidden):
                side = lax.dynamic_slice_in_dim(rows, which * piece, piece, axis=1)
                return lax.dot_general(side, hidden, over_rows, preferred_element_type=F32)

            return part(own_half, own_hidden) + part(rest_cots[h], rest_hidden)

        theirs = other_core(grad_of(1 - core).astype(BF16))
        done.append((grad_of(core) + theirs.astype(F32)).astype(BF16))
    return mixed, jnp.concatenate(done, axis=0)[None]


def solution(mesh):
    placed = (
        P(("groups", "expert", "dp"), None),
        P(("groups", "expert", "dp"), None),
        P(("groups", "expert", "dp"), None),
        P(("groups", "expert", "dp"), None),
        P("expert", "dp", None),
        P("expert", "dp", None),
        P("expert", "dp", None),
    )
    return jax.shard_map(
        shards,
        mesh=mesh,
        in_specs=placed,
        out_specs=(P(("groups", "expert", "dp"), None), P(("groups", "expert"), "dp", None)),
        check_vma=False,
    )
```

```python
import functools

import jax
import jax.numpy as jnp
from jax import lax
from jax.experimental import pallas as pl
from jax.experimental.pallas import tpu as pltpu
from jax.sharding import PartitionSpec as P

F32 = jnp.float32
BF16 = jnp.bfloat16
VMEM_LIMIT = 48 * 1024 * 1024


def two_levels(experts):
    minor = 1
    while minor * minor * 4 <= experts:
        minor *= 2
    return experts // minor, minor


def column_tile(columns):
    return 512 if columns % 512 == 0 else columns


def select_kernel(peers, count, slots, scaled, _, pos_ref, weight_ref, *refs):
    sources, outs = refs[:count], refs[count:]
    toks = pos_ref.shape[1]
    slot = lax.broadcasted_iota(jnp.int32, (slots, toks), 0).astype(F32)
    for g in range(count):
        hits = [slot == pos_ref[k * count + g : k * count + g + 1, :] for k in range(peers)]
        onehot = jnp.concatenate([jnp.where(h, 1.0, 0.0) for h in hits], axis=0).astype(BF16)
        rows = jnp.dot(onehot, sources[g][0], preferred_element_type=F32)
        for k in range(peers):
            part = rows[k * slots : (k + 1) * slots]
            if scaled:
                weights = weight_ref[k * count + g : k * count + g + 1, :]
                part = part * jnp.sum(jnp.where(hits[k], weights, 0.0), axis=1, keepdims=True)
            outs[k][g] = part.astype(BF16)


def select(blocks, which, table, slots, scaled, tiles, tile):
    pos, weight = table
    count = len(blocks)
    peers = pos.shape[0] // count
    toks = blocks[0].shape[1]
    cols = tile * len(tiles)
    small = pl.BlockSpec(pos.shape, lambda j, ref: (0, 0))
    step = tiles[1] - tiles[0] if len(tiles) > 1 else 1
    inner = next((i for i in range(1, len(tiles)) if tiles[i] - tiles[i - 1] != step), len(tiles))
    hop = tiles[inner] - tiles[0] if inner < len(tiles) else 0

    def column(j):
        return tiles[0] + lax.rem(j, inner) * step + (j // inner) * hop

    def source(g):
        return pl.BlockSpec((1, toks, tile), lambda j, ref: (ref[g], 0, column(j)))

    return pl.pallas_call(
        functools.partial(select_kernel, peers, count, slots, scaled),
        grid_spec=pltpu.PrefetchScalarGridSpec(
            num_scalar_prefetch=1,
            grid=(len(tiles),),
            in_specs=[small, small] + [source(g) for g in range(count)],
            out_specs=[pl.BlockSpec((count, slots, tile), lambda j, ref: (0, 0, j))] * peers,
        ),
        out_shape=[jax.ShapeDtypeStruct((count, slots, cols), BF16)] * peers,
        compiler_params=pltpu.CompilerParams(vmem_limit_bytes=VMEM_LIMIT),
        cost_estimate=pl.CostEstimate(
            flops=2 * peers * count * slots * toks * cols,
            bytes_accessed=2 * count * cols * (toks + peers * slots),
            transcendentals=0,
        ),
    )(which, pos, weight, *blocks)


def combine_kernel(peers, _, pos_ref, weight_ref, *refs):
    own, rest, out = refs[:peers], refs[peers : 2 * peers], refs[2 * peers]
    g, count = pl.program_id(0), pl.num_programs(0)
    toks, slots = pos_ref.shape[1], own[0].shape[1]

    def add_up(rows):
        slot = lax.broadcasted_iota(jnp.int32, (slots, toks), 0).astype(F32)
        spread = []
        for k in range(peers):
            at = pl.ds(k * count + g, 1)
            spread.append(jnp.where(slot == pos_ref[at, :], weight_ref[at, :], 0.0))
        spread = jnp.concatenate(spread, axis=0)
        high = spread.astype(BF16).astype(F32)
        both = jnp.concatenate([high, spread - high], axis=1).astype(BF16)
        held = jnp.concatenate([r[0] for r in rows], axis=0)
        total = lax.dot_general(both, held, (((0,), (0,)), ((), ())), preferred_element_type=F32)
        out[0] = (total[:toks] + total[toks:]).astype(BF16)

    pl.when(g == 0)(lambda: add_up(own))
    pl.when(g > 0)(lambda: add_up(rest))


def combine(which, table, own, rest, half):
    pos, weight = table
    count, slots, cols = rest[0].shape
    count += 1
    peers, toks = len(rest), pos.shape[1]
    small = pl.BlockSpec(pos.shape, lambda g, ref: (0, 0))
    return pl.pallas_call(
        functools.partial(combine_kernel, peers),
        grid_spec=pltpu.PrefetchScalarGridSpec(
            num_scalar_prefetch=1,
            grid=(count,),
            in_specs=[small, small]
            + [pl.BlockSpec((1, slots, cols), lambda g, ref: (0, 0, half))] * peers
            + [pl.BlockSpec((1, slots, cols), lambda g, ref: (jnp.maximum(g - 1, 0), 0, 0))] * peers,
            out_specs=pl.BlockSpec((1, toks, cols), lambda g, ref: (ref[g], 0, 0)),
        ),
        out_shape=jax.ShapeDtypeStruct((count, toks, cols), BF16),
        compiler_params=pltpu.CompilerParams(vmem_limit_bytes=VMEM_LIMIT),
        cost_estimate=pl.CostEstimate(
            flops=4 * peers * count * slots * toks * cols,
            bytes_accessed=2 * cols * count * (toks + peers * slots),
            transcendentals=0,
        ),
    )(which, pos, weight, *own, *rest)


def place_kernel(a_ref, b_ref, *refs):
    refs[-1][...] = (a_ref[...] + b_ref[...].astype(F32)).astype(BF16)


def place_sum(a, b, at, count, base):
    rows, cols = a.shape
    block = pl.BlockSpec((rows, cols), lambda i: (0, 0))
    given = [a, b] if base is None else [a, b, base]
    return pl.pallas_call(
        place_kernel,
        grid=(1,),
        in_specs=[block, block, pl.BlockSpec(memory_space=pl.ANY)][: len(given)],
        out_specs=pl.BlockSpec((rows, cols), lambda i: (at, 0)),
        out_shape=jax.ShapeDtypeStruct((count * rows, cols), BF16),
        input_output_aliases={} if base is None else {2: 0},
        compiler_params=pltpu.CompilerParams(vmem_limit_bytes=VMEM_LIMIT),
        cost_estimate=pl.CostEstimate(
            flops=rows * cols, bytes_accessed=8 * rows * cols, transcendentals=0
        ),
    )(*given)


def expert_kernel(peers, parts, held, mats, halves, joined_out, *refs):
    take = iter(refs)
    rows = [[next(take) for _ in range(peers)] for _ in range(parts)]
    gates, ups = ([next(take) for _ in range(mats)] for _ in range(2))
    before = [next(take) for _ in range(2)] if held else None
    downs = [next(take) for _ in range(halves)]
    outs = list(take)
    count, slots = rows[0][0].shape[:2]
    pieces = []
    for part in rows:
        stacked = jnp.concatenate([x[g] for x in part for g in range(count)], axis=0)
        deep = gates[0].shape[0]
        pieces += [stacked[:, at : at + deep] for at in range(0, stacked.shape[1], deep)]
    sums = []
    for i, mats in enumerate((gates, ups)):
        total = before[i][...] if before else None
        for x, w in zip(pieces, mats):
            part = jnp.dot(x, w[...], preferred_element_type=F32)
            total = part if total is None else total + part
        sums.append(total)
    if not halves:
        outs[0][...], outs[1][...] = sums
        return
    wider = sums[0] / (1.0 + jnp.exp(-sums[0])) * sums[1]
    for i in range(peers * count):
        outs[0][i] = wider[i * slots : (i + 1) * slots].astype(BF16)
    project(peers, count, slots, wider.astype(BF16), downs, outs[1:], joined_out)


def project(peers, count, slots, hidden, downs, outs, joined_out):
    for h, w in enumerate(downs):
        wide = w.shape[0]
        out = lax.dot_general(
            hidden, w[...], (((1,), (1,)), ((), ())), preferred_element_type=F32
        )
        for k in range(peers):
            for g in range(count):
                at = (k * count + g) * slots
                block = out[at : at + slots].astype(BF16)
                if joined_out:
                    outs[k][g, :, h * wide : (h + 1) * wide] = block
                else:
                    outs[k][g] = block


def project_kernel(peers, count, hidden_ref, down_ref, *outs):
    slots = hidden_ref.shape[1]
    hidden = jnp.concatenate([hidden_ref[i] for i in range(peers * count)], axis=0)
    project(peers, count, slots, hidden, [down_ref], outs, False)


def in_vmem(kernel, shapes, flops, *args):
    vmem = pl.BlockSpec(memory_space=pltpu.VMEM)
    return pl.pallas_call(
        kernel,
        in_specs=[vmem] * len(args),
        out_specs=[vmem] * len(shapes),
        out_shape=shapes,
        compiler_params=pltpu.CompilerParams(vmem_limit_bytes=VMEM_LIMIT),
        cost_estimate=pl.CostEstimate(
            flops=flops,
            bytes_accessed=sum(x.size * x.dtype.itemsize for x in (*args, *shapes)),
            transcendentals=0,
        ),
    )(*args)


def expert(rows, gates, ups, held, downs):
    peers = len(rows[0])
    count, slots, _ = rows[0][0].shape
    units = gates[0].shape[1]
    total = peers * count * slots
    flops = 4 * total * units * sum(w.shape[0] for w in gates)
    if not downs:
        shapes = [jax.ShapeDtypeStruct((total, units), F32)] * 2
    else:
        wide = sum(w.shape[0] for w in downs)
        flops += 2 * total * units * wide
        shapes = [jax.ShapeDtypeStruct((peers * count, slots, units), BF16)]
        shapes += [jax.ShapeDtypeStruct((count, slots, wide), BF16)] * peers
    kernel = functools.partial(
        expert_kernel, peers, len(rows), bool(held), len(gates), len(downs), len(downs) > 1
    )
    return in_vmem(kernel, shapes, flops, *sum(rows, []), *gates, *ups, *held, *downs)


def own_grad_kernel(peers, _, hidden_ref, *refs):
    rows = jnp.concatenate([x[0] for x in refs[:peers]], axis=0)
    hidden = jnp.concatenate([hidden_ref[k] for k in range(peers)], axis=0)
    refs[peers][0] = lax.dot_general(
        rows, hidden, (((0,), (0,)), ((), ())), preferred_element_type=F32
    )


def own_grads(blocks, hidden, rows, piece):
    peers, slots, units = hidden.shape
    count = blocks.shape[0]
    return pl.pallas_call(
        functools.partial(own_grad_kernel, peers),
        grid_spec=pltpu.PrefetchScalarGridSpec(
            num_scalar_prefetch=1,
            grid=(count,),
            in_specs=[pl.BlockSpec(hidden.shape, lambda i, ref: (0, 0, 0))]
            + [pl.BlockSpec((1, slots, piece), lambda i, ref: (0, 0, ref[i]))] * peers,
            out_specs=pl.BlockSpec((1, piece, units), lambda i, ref: (i, 0, 0)),
        ),
        out_shape=jax.ShapeDtypeStruct((count, piece, units), F32),
        compiler_params=pltpu.CompilerParams(vmem_limit_bytes=VMEM_LIMIT),
        cost_estimate=pl.CostEstimate(
            flops=2 * peers * slots * count * piece * units,
            bytes_accessed=4 * count * piece * units,
            transcendentals=0,
        ),
    )(blocks, hidden, *rows)


def shards(tokens, routes, route_logits, cotangent, gate_weight, up_weight, down_weight):
    toks, top = routes.shape
    experts = lax.axis_size("expert")
    major, minor = two_levels(experts)
    per_expert = toks * top // experts
    slots = min(toks, per_expert + max(2, per_expert // 8))
    slots = -(-slots // 8) * 8
    here = lax.axis_index("expert")
    core = lax.axis_index("dp")
    plane, place = here // minor, here % minor

    def to_plane(x, shift):
        return lax.ppermute(x, "expert", [(i, (i + shift * minor) % experts) for i in range(experts)])

    def to_peer(x, k):
        return lax.ppermute(x, "expert", [(i, i ^ k) for i in range(experts)])

    def other_core(x):
        return lax.ppermute(x, "dp", [(0, 1), (1, 0)])

    def after(x, earlier):
        return lax.optimization_barrier((x, *earlier))[0] if earlier else x

    def after_all(xs, earlier):
        return list(lax.optimization_barrier((*xs, *earlier))[: len(xs)])

    exp_logits = jnp.exp(route_logits)
    route_weight = (exp_logits / jnp.sum(exp_logits, axis=1, keepdims=True)).T
    names = routes.T[:, None, :] == jnp.arange(experts, dtype=jnp.int32)[None, :, None]
    chosen = jnp.sum(names.astype(F32), axis=0)
    dense_weight = jnp.sum(jnp.where(names, route_weight[:, None, :], 0.0), axis=0)
    before = jnp.arange(toks)[:, None] < jnp.arange(toks)[None, :]
    position = jnp.dot(chosen.astype(BF16), before.astype(BF16), preferred_element_type=F32)
    meta = jnp.stack([jnp.where(chosen > 0, position, -1.0), dense_weight])

    mine = plane * minor + (place ^ jnp.arange(minor))
    mine = (mine[:, None] == jnp.arange(experts)[None, :]).astype(F32)

    sender = (plane + major - jnp.arange(major, dtype=jnp.int32)) % major
    zero = jnp.zeros((1,), jnp.int32)
    same_place = [[i * minor + j for i in range(major)] for j in range(minor)]
    model_width, out_cols = tokens.shape[1], cotangent.shape[1]
    piece, wide, deep = out_cols // 4, out_cols // 2, model_width // 2

    def spread(x):
        return lax.all_gather(x, "expert", axis=0, axis_index_groups=same_place)

    token_all = [spread(tokens[:, h * deep : (h + 1) * deep]) for h in range(2)]
    cot_all = [
        spread(
            jnp.concatenate(
                [cotangent[:, i * piece : (i + 1) * piece] for i in (h, 2 + h)], axis=1
            )
        )
        for h in range(2)
    ]
    metas = [meta] + [to_plane(meta, s) for s in range(1, major)]

    def table_of(shifts):
        stacked = jnp.stack([metas[s] for s in shifts])
        picked = jnp.sum(stacked[:, :, None] * mine[None, None, :, :, None], axis=3)
        picked = picked.transpose(1, 2, 0, 3).reshape(2, minor * len(shifts), toks)
        return picked[0], picked[1]

    own_table, all_table = table_of([0]), table_of(list(range(major)))
    rest_table = [t.reshape(minor, major, toks)[:, 1:].reshape(-1, toks) for t in all_table]

    queue = [[] for _ in range(minor)]

    def exchange(rows):
        back = [rows[0]]
        for k in range(1, minor):
            back.append(to_peer(after(rows[k], queue[k]), k))
            queue[k] = [back[k]]
        return back

    def pick_rest(x, scaled):
        tile = column_tile(x.shape[2])
        tiles = list(range(x.shape[2] // tile))
        return select([x] * (major - 1), sender[1:], rest_table, slots, scaled, tiles, tile)

    tile = column_tile(model_width)
    got = [other_core(w[0]) for w in (gate_weight, up_weight, down_weight)]
    gate_mats, up_mats, down_mats = (
        [jnp.where(core == 0, w[0], g), jnp.where(core == 0, g, w[0])]
        for w, g in zip((gate_weight, up_weight, down_weight), got)
    )
    every = list(range(model_width // tile))
    own_tokens = after(tokens, metas[1:])[None]
    own_rows = exchange(select([own_tokens], zero, own_table, slots, False, every, tile))
    own_cots = exchange(
        select([cotangent[None]], zero, own_table, slots, True, [0, 2, 1, 3], piece)
    )
    first = exchange(pick_rest(after(token_all[0], got), False))
    second = exchange(pick_rest(after(token_all[1], first[1:]), False))
    own_hidden, *own_out = expert([own_rows], gate_mats, up_mats, [], down_mats)
    held = expert([first], gate_mats[:1], up_mats[:1], [], [])
    own_back = exchange(after_all(own_out, held))
    rest_hidden, *out = expert([second], gate_mats[1:], up_mats[1:], held, down_mats[:1])

    shapes = [jax.ShapeDtypeStruct(x.shape, x.dtype) for x in out]
    flops = 2 * rest_hidden.size * wide
    kernel = functools.partial(project_kernel, minor, major - 1)
    outs = [out, in_vmem(kernel, shapes, flops, rest_hidden, down_mats[1])]
    cots = [pick_rest(after(cot_all[0], out[1:]), True), None]
    mixed = []
    for h in range(2):
        back = exchange(outs[h] if h else after_all(outs[h], cots[0]))
        sums = combine(sender, all_table, own_back, after_all(back, outs[1]), h)
        mixed.append(
            lax.psum_scatter(sums, "expert", scatter_dimension=0, axis_index_groups=same_place)
        )
    mixed = jnp.concatenate(mixed, axis=1)
    cots[1] = pick_rest(cot_all[1], True)
    rest_cots = [exchange(x) for x in cots]

    whose = (1 - core, core)
    blocks = jnp.stack([2 * h + c for h in range(2) for c in whose]).astype(jnp.int32)
    own_parts = own_grads(blocks, own_hidden, own_cots, piece)
    rest_hidden = rest_hidden.reshape(-1, rest_hidden.shape[2])
    grad = None
    for h in range(2):
        rows = jnp.concatenate(rest_cots[h], axis=0).reshape(-1, wide)
        theirs, ours = (
            own_parts[2 * h + i]
            + lax.dot_general(
                lax.dynamic_slice_in_dim(rows, c * piece, piece, axis=1),
                rest_hidden,
                (((0,), (0,)), ((), ())),
                preferred_element_type=F32,
            )
            for i, c in enumerate(whose)
        )
        theirs = other_core(theirs.astype(BF16))
        grad = place_sum(ours, after(theirs, [mixed] if h else []), h, 2, grad)
    return mixed, grad[None]


def solution(mesh):
    placed = (
        P(("groups", "expert", "dp"), None),
        P(("groups", "expert", "dp"), None),
        P(("groups", "expert", "dp"), None),
        P(("groups", "expert", "dp"), None),
        P("expert", "dp", None),
        P("expert", "dp", None),
        P("expert", "dp", None),
    )
    return jax.shard_map(
        shards,
        mesh=mesh,
        in_specs=placed,
        out_specs=(P(("groups", "expert", "dp"), None), P(("groups", "expert"), "dp", None)),
        check_vma=False,
    )
```

```python
import functools

import jax
import jax.numpy as jnp
from jax import lax
from jax.experimental import pallas as pl
from jax.experimental.pallas import tpu as pltpu
from jax.sharding import PartitionSpec as P

F32 = jnp.float32
BF16 = jnp.bfloat16
VMEM_LIMIT = 32 * 1024 * 1024
LONG = pl.CostEstimate(flops=10**11, bytes_accessed=1, transcendentals=0)


def two_levels(experts):
    minor = 1
    while minor * minor * 4 <= experts:
        minor *= 2
    return experts // minor, minor


def column_tile(columns):
    return next((t for t in (512, 640, 384) if columns % t == 0), columns)


def select_kernel(peers, count, slots, scaled, _, pos_ref, weight_ref, *refs):
    sources, outs = refs[:count], refs[count:]
    toks = pos_ref.shape[1]
    slot = lax.broadcasted_iota(jnp.int32, (slots, toks), 0).astype(F32)
    for g in range(count):
        hits = [slot == pos_ref[k * count + g : k * count + g + 1, :] for k in range(peers)]
        onehot = jnp.concatenate([jnp.where(h, 1.0, 0.0) for h in hits], axis=0).astype(BF16)
        rows = jnp.dot(onehot, sources[g][0], preferred_element_type=F32)
        for k in range(peers):
            part = rows[k * slots : (k + 1) * slots]
            if scaled:
                weights = weight_ref[k * count + g : k * count + g + 1, :]
                part = part * jnp.sum(jnp.where(hits[k], weights, 0.0), axis=1, keepdims=True)
            outs[k][g] = part.astype(BF16)


def select(blocks, which, table, slots, scaled, tiles, tile):
    pos, weight = table
    count = len(blocks)
    peers = pos.shape[0] // count
    toks = blocks[0].shape[1]
    cols = tile * len(tiles)
    small = pl.BlockSpec(pos.shape, lambda j, ref: (0, 0))
    step = tiles[1] - tiles[0] if len(tiles) > 1 else 1
    inner = next((i for i in range(1, len(tiles)) if tiles[i] - tiles[i - 1] != step), len(tiles))
    hop = tiles[inner] - tiles[0] if inner < len(tiles) else 0

    def column(j):
        return tiles[0] + lax.rem(j, inner) * step + (j // inner) * hop

    def source(g):
        return pl.BlockSpec((1, toks, tile), lambda j, ref: (ref[g], 0, column(j)))

    return pl.pallas_call(
        functools.partial(select_kernel, peers, count, slots, scaled),
        grid_spec=pltpu.PrefetchScalarGridSpec(
            num_scalar_prefetch=1,
            grid=(len(tiles),),
            in_specs=[small, small] + [source(g) for g in range(count)],
            out_specs=[pl.BlockSpec((count, slots, tile), lambda j, ref: (0, 0, j))] * peers,
        ),
        out_shape=[jax.ShapeDtypeStruct((count, slots, cols), BF16)] * peers,
        compiler_params=pltpu.CompilerParams(vmem_limit_bytes=VMEM_LIMIT),
        cost_estimate=pl.CostEstimate(
            flops=2 * peers * count * slots * toks * cols,
            bytes_accessed=2 * count * cols * (toks + peers * slots),
            transcendentals=0,
        ),
    )(which, pos, weight, *blocks)


def combine_kernel(peers, _, pos_ref, weight_ref, *refs):
    own, rest, out = refs[:peers], refs[peers : 2 * peers], refs[2 * peers]
    g, count = pl.program_id(0), pl.num_programs(0)
    toks, slots = pos_ref.shape[1], own[0].shape[1]

    def add_up(rows):
        slot = lax.broadcasted_iota(jnp.int32, (slots, toks), 0).astype(F32)
        spread = []
        for k in range(peers):
            at = pl.ds(k * count + g, 1)
            spread.append(jnp.where(slot == pos_ref[at, :], weight_ref[at, :], 0.0))
        spread = jnp.concatenate(spread, axis=0)
        high = spread.astype(BF16).astype(F32)
        both = jnp.concatenate([high, spread - high], axis=1).astype(BF16)
        held = jnp.concatenate([r[0] for r in rows], axis=0)
        total = lax.dot_general(both, held, (((0,), (0,)), ((), ())), preferred_element_type=F32)
        out[0] = (total[:toks] + total[toks:]).astype(BF16)

    pl.when(g == 0)(lambda: add_up(own))
    pl.when(g > 0)(lambda: add_up(rest))


def combine(which, table, own, rest, half):
    pos, weight = table
    count, slots, cols = rest[0].shape
    count += 1
    peers, toks = len(rest), pos.shape[1]
    small = pl.BlockSpec(pos.shape, lambda g, ref: (0, 0))
    return pl.pallas_call(
        functools.partial(combine_kernel, peers),
        grid_spec=pltpu.PrefetchScalarGridSpec(
            num_scalar_prefetch=1,
            grid=(count,),
            in_specs=[small, small]
            + [pl.BlockSpec((1, slots, cols), lambda g, ref: (0, 0, half))] * peers
            + [pl.BlockSpec((1, slots, cols), lambda g, ref: (jnp.maximum(g - 1, 0), 0, 0))] * peers,
            out_specs=pl.BlockSpec((1, toks, cols), lambda g, ref: (ref[g], 0, 0)),
        ),
        out_shape=jax.ShapeDtypeStruct((count, toks, cols), BF16),
        compiler_params=pltpu.CompilerParams(vmem_limit_bytes=VMEM_LIMIT),
        cost_estimate=LONG,
    )(which, pos, weight, *own, *rest)


def place_kernel(a_ref, b_ref, *refs):
    refs[-1][...] = (a_ref[...] + b_ref[...].astype(F32)).astype(BF16)


def place_sum(a, b, at, count, base):
    rows, cols = a.shape
    block = pl.BlockSpec((rows, cols), lambda i: (0, 0))
    given = [a, b] if base is None else [a, b, base]
    return pl.pallas_call(
        place_kernel,
        grid=(1,),
        in_specs=[block, block, pl.BlockSpec(memory_space=pl.ANY)][: len(given)],
        out_specs=pl.BlockSpec((rows, cols), lambda i: (at, 0)),
        out_shape=jax.ShapeDtypeStruct((count * rows, cols), BF16),
        input_output_aliases={} if base is None else {2: 0},
        compiler_params=pltpu.CompilerParams(vmem_limit_bytes=VMEM_LIMIT),
        cost_estimate=pl.CostEstimate(
            flops=rows * cols, bytes_accessed=8 * rows * cols, transcendentals=0
        ),
    )(*given)


def expert_kernel(peers, spans, held, mats, halves, joined_out, *refs):
    take = iter(refs)
    rows = [next(take) for _ in range(peers)]
    gates, ups = ([next(take) for _ in range(mats)] for _ in range(2))
    before = [next(take) for _ in range(2)] if held else None
    downs = [next(take) for _ in range(halves)]
    outs = list(take)
    count, slots = rows[0].shape[:2]
    stacked = jnp.concatenate([x[g] for x in rows for g in range(count)], axis=0)
    sums = []
    for i, weights in enumerate((gates, ups)):
        total, at = before[i][...] if before else None, 0
        for which, low, high in spans:
            piece = stacked[:, at : at + high - low]
            part = jnp.dot(piece, weights[which][low:high], preferred_element_type=F32)
            total, at = part if total is None else total + part, at + high - low
        sums.append(total)
    if not halves:
        outs[0][...], outs[1][...] = sums
        return
    wider = sums[0] / (1.0 + jnp.exp(-sums[0])) * sums[1]
    for i in range(peers * count):
        outs[0][i] = wider[i * slots : (i + 1) * slots].astype(BF16)
    project(peers, count, slots, wider.astype(BF16), downs, outs[1:], joined_out)


def project(peers, count, slots, hidden, downs, outs, joined_out):
    for h, w in enumerate(downs):
        wide = w.shape[0]
        out = lax.dot_general(
            hidden, w[...], (((1,), (1,)), ((), ())), preferred_element_type=F32
        )
        for k in range(peers):
            for g in range(count):
                at = (k * count + g) * slots
                block = out[at : at + slots].astype(BF16)
                if joined_out:
                    outs[k][g, :, h * wide : (h + 1) * wide] = block
                else:
                    outs[k][g] = block


def project_kernel(peers, count, hidden_ref, down_ref, *outs):
    slots = hidden_ref.shape[1]
    hidden = jnp.concatenate([hidden_ref[i] for i in range(peers * count)], axis=0)
    project(peers, count, slots, hidden, [down_ref], outs, False)


def in_vmem(kernel, shapes, flops, *args):
    vmem = pl.BlockSpec(memory_space=pltpu.VMEM)
    return pl.pallas_call(
        kernel,
        in_specs=[vmem] * len(args),
        out_specs=[vmem] * len(shapes),
        out_shape=shapes,
        compiler_params=pltpu.CompilerParams(vmem_limit_bytes=VMEM_LIMIT),
        cost_estimate=pl.CostEstimate(
            flops=flops,
            bytes_accessed=sum(x.size * x.dtype.itemsize for x in (*args, *shapes)),
            transcendentals=0,
        ),
    )(*args)


def expert(rows, spans, gates, ups, held, downs):
    peers = len(rows)
    count, slots, deep = rows[0].shape
    units = gates[0].shape[1]
    total = peers * count * slots
    flops = 4 * total * units * deep
    if not downs:
        shapes = [jax.ShapeDtypeStruct((total, units), F32)] * 2
    else:
        wide = sum(w.shape[0] for w in downs)
        flops += 2 * total * units * wide
        shapes = [jax.ShapeDtypeStruct((peers * count, slots, units), BF16)]
        shapes += [jax.ShapeDtypeStruct((count, slots, wide), BF16)] * peers
    kernel = functools.partial(
        expert_kernel, peers, spans, bool(held), len(gates), len(downs), len(downs) > 1
    )
    return in_vmem(kernel, shapes, flops, *rows, *gates, *ups, *held, *downs)


def own_grad_kernel(peers, _, hidden_ref, *refs):
    rows = jnp.concatenate([x[0] for x in refs[:peers]], axis=0)
    hidden = jnp.concatenate([hidden_ref[k] for k in range(peers)], axis=0)
    refs[peers][0] = lax.dot_general(
        rows, hidden, (((0,), (0,)), ((), ())), preferred_element_type=F32
    )


def own_grads(blocks, hidden, rows, piece):
    peers, slots, units = hidden.shape
    count = blocks.shape[0]
    return pl.pallas_call(
        functools.partial(own_grad_kernel, peers),
        grid_spec=pltpu.PrefetchScalarGridSpec(
            num_scalar_prefetch=1,
            grid=(count,),
            in_specs=[pl.BlockSpec(hidden.shape, lambda i, ref: (0, 0, 0))]
            + [pl.BlockSpec((1, slots, piece), lambda i, ref: (0, 0, ref[i]))] * peers,
            out_specs=pl.BlockSpec((1, piece, units), lambda i, ref: (i, 0, 0)),
        ),
        out_shape=jax.ShapeDtypeStruct((count, piece, units), F32),
        compiler_params=pltpu.CompilerParams(vmem_limit_bytes=VMEM_LIMIT),
        cost_estimate=LONG,
    )(blocks, hidden, *rows)


def shards(tokens, routes, route_logits, cotangent, gate_weight, up_weight, down_weight):
    toks, top = routes.shape
    experts = lax.axis_size("expert")
    major, minor = two_levels(experts)
    per_expert = toks * top // experts
    slots = min(toks, per_expert + max(2, per_expert // 8))
    slots = -(-slots // 8) * 8
    here = lax.axis_index("expert")
    core = lax.axis_index("dp")
    plane, place = here // minor, here % minor

    def to_plane(x, shift):
        return lax.ppermute(x, "expert", [(i, (i + shift * minor) % experts) for i in range(experts)])

    def to_peer(x, k):
        return lax.ppermute(x, "expert", [(i, i ^ k) for i in range(experts)])

    def other_core(x):
        return lax.ppermute(x, "dp", [(0, 1), (1, 0)])

    def after(x, earlier):
        return lax.optimization_barrier((x, *earlier))[0] if earlier else x

    def after_all(xs, earlier):
        return list(lax.optimization_barrier((*xs, *earlier))[: len(xs)])

    exp_logits = jnp.exp(route_logits)
    route_weight = (exp_logits / jnp.sum(exp_logits, axis=1, keepdims=True)).T
    names = routes.T[:, None, :] == jnp.arange(experts, dtype=jnp.int32)[None, :, None]
    chosen = jnp.sum(names.astype(F32), axis=0)
    dense_weight = jnp.sum(jnp.where(names, route_weight[:, None, :], 0.0), axis=0)
    before = jnp.arange(toks)[:, None] < jnp.arange(toks)[None, :]
    position = jnp.dot(chosen.astype(BF16), before.astype(BF16), preferred_element_type=F32)
    meta = jnp.stack([jnp.where(chosen > 0, position, -1.0), dense_weight])

    mine = plane * minor + (place ^ jnp.arange(minor))
    mine = (mine[:, None] == jnp.arange(experts)[None, :]).astype(F32)

    sender = (plane + major - jnp.arange(major, dtype=jnp.int32)) % major
    zero = jnp.zeros((1,), jnp.int32)
    same_place = [[i * minor + j for i in range(major)] for j in range(minor)]
    model_width, out_cols = tokens.shape[1], cotangent.shape[1]
    piece, wide, deep = out_cols // 4, out_cols // 2, model_width // 2

    def spread(x):
        return lax.all_gather(x, "expert", axis=0, axis_index_groups=same_place)

    cut = model_width // 2
    token_all = [spread(tokens[:, :cut]), spread(tokens[:, cut:])]
    cot_all = spread(cotangent)
    metas = [meta] + [to_plane(meta, s) for s in range(1, major)]

    def table_of(shifts):
        stacked = jnp.stack([metas[s] for s in shifts])
        picked = jnp.sum(stacked[:, :, None] * mine[None, None, :, :, None], axis=3)
        picked = picked.transpose(1, 2, 0, 3).reshape(2, minor * len(shifts), toks)
        return picked[0], picked[1]

    own_table, all_table = table_of([0]), table_of(list(range(major)))
    rest_table = [t.reshape(minor, major, toks)[:, 1:].reshape(-1, toks) for t in all_table]

    queue = [[] for _ in range(minor)]

    def exchange(rows):
        back = [rows[0]]
        for k in range(1, minor):
            back.append(to_peer(after(rows[k], queue[k]), k))
            queue[k] = [back[k]]
        return back

    def pick_rest(x, scaled, tiles, tile):
        return select([x] * (major - 1), sender[1:], rest_table, slots, scaled, tiles, tile)

    def pick_tokens(x):
        tile = column_tile(x.shape[2])
        return pick_rest(x, False, list(range(x.shape[2] // tile)), tile)

    tile = column_tile(model_width)
    got = [other_core(w[0]) for w in (gate_weight, up_weight, down_weight)]
    gate_mats, up_mats, down_mats = (
        [jnp.where(core == 0, w[0], g), jnp.where(core == 0, g, w[0])]
        for w, g in zip((gate_weight, up_weight, down_weight), got)
    )
    every = list(range(model_width // tile))
    own_tokens = after(tokens, metas[1:])[None]
    own_rows = exchange(select([own_tokens], zero, own_table, slots, False, every, tile))
    own_cots = exchange(
        select([cotangent[None]], zero, own_table, slots, True, [0, 2, 1, 3], piece)
    )
    first = exchange(pick_tokens(after(token_all[0], got)))
    second = exchange(pick_tokens(after(token_all[1], first[1:])))
    both = [(0, 0, deep), (1, 0, deep)]
    own_hidden, *own_out = expert(own_rows, both, gate_mats, up_mats, [], down_mats)
    early = [(0, 0, deep)]
    held = expert(first, early, gate_mats[:1], up_mats[:1], [], [])
    own_back = exchange(after_all(own_out, held))
    late = [(0, 0, deep)]
    rest_hidden, *out = expert(second, late, gate_mats[1:], up_mats[1:], held, down_mats[:1])

    shapes = [jax.ShapeDtypeStruct(x.shape, x.dtype) for x in out]
    flops = 2 * rest_hidden.size * wide
    kernel = functools.partial(project_kernel, minor, major - 1)
    outs = [out, in_vmem(kernel, shapes, flops, rest_hidden, down_mats[1])]
    cots = [None, None]
    mixed = []
    for h in range(2):
        back = exchange(outs[h])
        cots[h] = pick_rest(after(cot_all, back[1:] if h else out[1:]), True, [h, 2 + h], piece)
        sums = combine(sender, all_table, own_back, after_all(back, [] if h else [*outs[1], *cots[0]]), h)
        mixed.append(
            lax.psum_scatter(sums, "expert", scatter_dimension=0, axis_index_groups=same_place)
        )
    mixed = jnp.concatenate(mixed, axis=1)
    rest_cots = [exchange(x) for x in cots]

    whose = (1 - core, core)
    blocks = jnp.stack([2 * h + c for h in range(2) for c in whose]).astype(jnp.int32)
    own_cots = after_all(own_cots, rest_cots[0][1:])
    own_parts = own_grads(blocks, own_hidden, own_cots, piece)
    rest_hidden = rest_hidden.reshape(-1, rest_hidden.shape[2])
    grad = None
    for h in range(2):
        rows = jnp.concatenate(rest_cots[h], axis=0).reshape(-1, wide)
        theirs, ours = (
            own_parts[2 * h + i]
            + lax.dot_general(
                lax.dynamic_slice_in_dim(rows, c * piece, piece, axis=1),
                rest_hidden,
                (((0,), (0,)), ((), ())),
                preferred_element_type=F32,
            )
            for i, c in enumerate(whose)
        )
        theirs = other_core(theirs.astype(BF16))
        grad = place_sum(ours, after(theirs, [mixed] if h else []), h, 2, grad)
    return mixed, grad[None]


def solution(mesh):
    placed = (
        P(("groups", "expert", "dp"), None),
        P(("groups", "expert", "dp"), None),
        P(("groups", "expert", "dp"), None),
        P(("groups", "expert", "dp"), None),
        P("expert", "dp", None),
        P("expert", "dp", None),
        P("expert", "dp", None),
    )
    return jax.shard_map(
        shards,
        mesh=mesh,
        in_specs=placed,
        out_specs=(P(("groups", "expert", "dp"), None), P(("groups", "expert"), "dp", None)),
        check_vma=False,
    )
```
